128 devices in a mesh: row: 8 (over x, z_lo), col: 16 (over y, z_hi, core).
Axes of the slice: x: 4, y: 4, z: 4 (z_hi: 2, z_lo: 2; z = z_hi * 2 + z_lo), core: 2. Of those that a mesh axis runs over, the one named last changes fastest.
Arguments:
- patch_rows: bfloat16 [131072, 1152], P(('row', 'col')), may hold values from -6 to 6
- segment_ids: int32 [128, 1024], P(('row', 'col')), may hold values from 0 to 7, never falling along the last dimension, each value on 1 to 256 neighbouring positions
- norm_gain: float32 [1152], replicated, may hold values from 0.25 to 1.75
- query_weight: bfloat16 [1152, 1152], P('col')
- key_weight: bfloat16 [1152, 1152], P('col')
- value_weight: bfloat16 [1152, 1152], P('col'), may hold values from -0.1875 to 0.1875
- out_weight: bfloat16 [1152, 1152], P('col'), may hold values from -0.1875 to 0.1875
- text_embeds: bfloat16 [1024, 1152], P(('row', 'col')), may hold values from -6 to 6
Outputs:
- encoded: bfloat16 [131072, 1152], P(('row', 'col'))
- image_grad: float32 [1024, 1152], P(('row', 'col'))
- text_grad: float32 [1024, 1152], P(('row', 'col'))
The draws below stay inside these ranges and needn't reach their ends.
Inputs may be any that keep to these rules, and one draw needn't show every extreme that they name: `segment_ids`: within each packed sequence the image numbers never fall, every image 0 to 7 appears with 1 to 256 rows, and some image of every sequence has exactly 256 rows.
All inputs are finite; a program needn't handle non-finite values.
Results may differ from the reference program's by a relative error of at most 0.0095.
Values may be sent and summed in bfloat16 or wider, within the bound.
No kernel may reach another device: no remote copies, remote signals or barrier semaphores. Data moves between devices by JAX's collectives and lax.ppermute only.
A program may use at most 192 MiB of HBM per device.

```python
import math
import jax
import jax.numpy as jnp
import numpy as np
from jax import lax

D = 1152
HEADS = 16
ROWS_DEV = 1024
IMG_DEV = 8
MOST_PATCH = 256
DEVICES_ALL = 128
TOKENS = 131072
NIMG = 1024


def shared_matrix(key):
    return jax.random.normal(key, (D, D), jnp.float32) * D ** (-0.5)


def draw_query_weight(key, part):
    base = shared_matrix(key)
    return base.astype(jnp.bfloat16)


def draw_key_weight(key, part):
    key = jax.random.fold_in(key, 5)
    fresh = jax.random.normal(key, (D, D), jnp.float32) * D ** (-0.5)
    return fresh.astype(jnp.bfloat16)


def block_levels(stream_key, extent, shards, least, top_value):
    factor_of, own = 1.0, jax.random.fold_in(stream_key, 6)
    for axis_at, shards_of in shards:
        steps = jnp.exp(jax.random.uniform(jax.random.fold_in(own, axis_at), (shards_of,), jnp.float32, least / len(shards), top_value / len(shards)))
        factor_of = factor_of * jnp.repeat(steps, extent[axis_at] // shards_of).reshape([-1 if axis == axis_at else 1 for axis in range(len(extent))])
    return factor_of


def profile(amount, total, limit, skew):
    portions = [(1 << 20) // math.isqrt(standing ** skew) + 1 for standing in range(2, amount + 1)]
    surplus, holding = total - limit - (amount - 1), [1] * (amount - 1)
    while surplus > 0:
        candidates = [i for i in range(amount - 1) if holding[i] < limit]
        whole, budget = sum([portions[i] for i in candidates]), surplus
        for i in candidates:
            addition = min(limit - holding[i], max(1, budget * portions[i] // whole), surplus)
            holding[i] = holding[i] + addition
            surplus = surplus - addition
    return np.array([limit] + holding)


def ragged(stream_key, count, total, most, slope):
    if count == 2:
        one = jax.random.randint(stream_key, (), max(1, total - most), min(most, total - 1) + 1)
        return jnp.stack([one, total - one])
    lengths = jnp.asarray(profile(count, total, most, slope), jnp.int32)
    twos = (count - 1) // 2
    donor, sink = lengths[1:1 + 2 * twos:2], lengths[2:2 + 2 * twos:2]
    margin = jnp.minimum(donor - 1, most - sink)
    shifted = jax.random.randint(jax.random.fold_in(stream_key, 1), (twos,), 0, 1 << 20) % (margin + 1)
    lengths = lengths.at[1:1 + 2 * twos:2].set(donor - shifted).at[2:2 + 2 * twos:2].set(sink + shifted)
    return lengths[jax.random.permutation(jax.random.fold_in(stream_key, 2), count)]


def centred(own_key, shape, scale, limit, cuts=(), kind=jnp.bfloat16):
    values = jax.random.normal(own_key, shape, jnp.float32) * scale
    if len(cuts) > 0:
        values = block_levels(own_key, shape, cuts, -0.22, 0.18) * values
    return jnp.clip(values, min=-limit, max=limit).astype(kind)


def setup_inputs(seed: int = 0) -> dict:
    key_list = jax.random.split(jax.random.key(seed), 9)
    patch_rows = centred(key_list[0], (TOKENS, D), 1.0, 6.0, ((0, 128),))
    segment_ids = jax.vmap(lambda own: jnp.searchsorted(jnp.cumsum(ragged(own, IMG_DEV, ROWS_DEV, MOST_PATCH, 2)), jnp.arange(ROWS_DEV), side="right"))(jax.random.split(key_list[1], DEVICES_ALL)).reshape((DEVICES_ALL, ROWS_DEV)).astype(jnp.int32)
    norm_gain = jnp.clip(1.0 + 0.15 * jax.random.normal(key_list[2], (D,), jnp.float32), 0.25, 1.75)
    query_weight = draw_query_weight(jax.random.fold_in(key_list[8], 71), 0)
    key_weight = draw_key_weight(jax.random.fold_in(key_list[8], 71), 0)
    value_weight = centred(key_list[5], (D, D), D ** -0.5, 0.1875, ((0, 16),))
    out_weight = centred(key_list[6], (D, D), D ** -0.5, 0.1875, ((0, 16),))
    text_embeds = centred(key_list[7], (NIMG, D), 1.0, 6.0, ((0, 128),))
    return dict(patch_rows=patch_rows, segment_ids=segment_ids, norm_gain=norm_gain, query_weight=query_weight, key_weight=key_weight, value_weight=value_weight, out_weight=out_weight, text_embeds=text_embeds)


def encode_one(rows, segs, gain, query_weight, key_weight, value_weight, out_weight):
    width = rows.shape[1]
    count = rows.shape[0]
    head_dim = width // HEADS
    xf = rows.astype(jnp.float32)
    centre = xf - lax.optimization_barrier(jnp.mean(xf, axis=1, keepdims=True))
    spread = lax.optimization_barrier(jnp.mean(centre * centre, axis=1, keepdims=True))
    normed = (centre * lax.rsqrt(spread + 1e-06) * gain).astype(jnp.bfloat16)
    queries = jnp.dot(normed, query_weight, preferred_element_type=jnp.float32).astype(jnp.bfloat16)
    keys = jnp.dot(normed, key_weight, preferred_element_type=jnp.float32).astype(jnp.bfloat16)
    values = jnp.dot(normed, value_weight, preferred_element_type=jnp.float32).astype(jnp.bfloat16)
    qh = queries.reshape(count, HEADS, head_dim).astype(jnp.float32)
    kh = keys.reshape(count, HEADS, head_dim).astype(jnp.float32)
    vh = values.reshape(count, HEADS, head_dim).astype(jnp.float32)
    scores = jnp.einsum('qhd,khd->hqk', qh, kh) / jnp.sqrt(jnp.float32(head_dim))
    same = segs[:, None] == segs[None, :]
    scores = jnp.where(same[None], scores, jnp.float32(-1e+30))
    top = lax.optimization_barrier(jnp.max(scores, axis=2, keepdims=True))
    expo = jnp.exp(scores - top)
    probs = (expo / lax.optimization_barrier(jnp.sum(expo, axis=2, keepdims=True))).astype(jnp.bfloat16)
    context = jnp.einsum('hqk,khd->qhd', probs.astype(jnp.float32), vh).astype(jnp.bfloat16).reshape(count, width)
    attended = jnp.dot(context, out_weight, preferred_element_type=jnp.float32)
    encoded = (xf + attended).astype(jnp.bfloat16)
    onehot = (segs[None, :] == jnp.arange(IMG_DEV, dtype=jnp.int32)[:, None]).astype(jnp.float32)
    sums = jnp.dot(onehot, encoded.astype(jnp.float32), precision=lax.Precision.HIGHEST)
    pooled = sums / lax.optimization_barrier(jnp.sum(onehot, axis=1, keepdims=True))
    unit = pooled * lax.rsqrt(lax.optimization_barrier(jnp.sum(pooled * pooled, axis=1, keepdims=True)) + 1e-06)
    return (encoded, unit)

def reference(patch_rows, segment_ids, norm_gain, query_weight, key_weight, value_weight, out_weight, text_embeds):
    seqs = segment_ids.shape[0]
    width = patch_rows.shape[1]
    packed = patch_rows.reshape(seqs, ROWS_DEV, width)

    def one(item):
        return encode_one(item[0], item[1], norm_gain, query_weight, key_weight, value_weight, out_weight)
    encoded, units = lax.map(one, (packed, segment_ids))
    encoded = encoded.reshape(seqs * ROWS_DEV, width)
    image_unit = units.reshape(seqs * IMG_DEV, width)
    tf = text_embeds.astype(jnp.float32)
    text_unit = tf * lax.rsqrt(lax.optimization_barrier(jnp.sum(tf * tf, axis=1, keepdims=True)) + 1e-06)
    total = image_unit.shape[0]
    logits = 10.0 * jnp.dot(image_unit, text_unit.T, precision=lax.Precision.HIGHEST) - 3.0
    sign = 2.0 * jnp.eye(total, dtype=jnp.float32) - 1.0
    coeffs = -sign * jax.nn.sigmoid(-sign * logits)
    image_grad = 10.0 * jnp.dot(coeffs, text_unit, precision=lax.Precision.HIGHEST)
    text_grad = 10.0 * jnp.dot(coeffs.T, image_unit, precision=lax.Precision.HIGHEST)
    return (encoded, image_grad, text_grad)
```

```python
import math

import jax
import jax.numpy as jnp
from jax import lax
from jax.experimental import pallas as pl
from jax.experimental.pallas import tpu as pltpu
from jax.sharding import PartitionSpec as P

HEADS = 16
IMG_DEV = 8
MASKED = -1e30
QUERY_ROWS = 256
KEY_ROWS = 128
F32 = jnp.float32
BF16 = jnp.bfloat16
VMEM = pl.BlockSpec(memory_space=pltpu.VMEM)
SMEM = pl.BlockSpec(memory_space=pltpu.SMEM)
BIG = pltpu.CompilerParams(vmem_limit_bytes=58 * 2**20)


def norm_kernel(x_ref, gain_ref, seg_ref, normed_ref, query_mark_ref, key_mark_ref):
    count = x_ref.shape[0]

    def one(i, _):
        rows = pl.ds(pl.multiple_of(i * 128, 128), 128)
        xf = x_ref[rows, :].astype(F32)
        centre = xf - jnp.mean(xf, axis=1, keepdims=True)
        spread = jnp.mean(centre * centre, axis=1, keepdims=True)
        normed_ref[rows, :] = (centre * lax.rsqrt(spread + 1e-06) * gain_ref[...]).astype(BF16)
        mine = seg_ref[rows, :] == lax.broadcasted_iota(jnp.int32, (128, 256), 1) % IMG_DEV
        query_mark_ref[rows, :] = jnp.where(mine, 1.0, 0.0).astype(BF16)
        key_mark_ref[rows, :] = jnp.where(mine, 0.0, MASKED).astype(BF16)
        return 0

    lax.fori_loop(0, count // 128, one, 0)


def norm(x, gain, segs):
    count, width = x.shape
    return pl.pallas_call(
        norm_kernel,
        out_shape=(
            jax.ShapeDtypeStruct((count, width), BF16),
            jax.ShapeDtypeStruct((count, 256), BF16),
            jax.ShapeDtypeStruct((count, 256), BF16),
        ),
        in_specs=[VMEM] * 3,
        out_specs=(VMEM,) * 3,
        compiler_params=BIG,
        name="norm",
    )(x, gain.reshape(1, width), segs.reshape(count, 1))


def attend_kernel(
    x_ref, normed_ref, query_mark_ref, key_mark_ref, segs_ref, window_ref, weight_ref,
    context_ref, rows_sum_ref, context_sum_ref, q_s, k_s, v_s,
):
    count, width = normed_ref.shape
    head_dim = width // HEADS
    scale = math.log2(math.e) / math.sqrt(head_dim)

    def project(i, _):
        rows = pl.ds(pl.multiple_of(i * 256, 256), 256)
        normed = normed_ref[rows, :]

        def one(at):
            return jnp.dot(normed, weight_ref[:, at * width : (at + 1) * width], preferred_element_type=F32)

        q_s[rows, :] = (one(0) * scale).astype(BF16)
        k_s[rows, :] = one(1).astype(BF16)
        v_s[rows, :] = one(2).astype(BF16)
        return 0

    lax.fori_loop(0, count // 256, project, 0)
    lane = lax.broadcasted_iota(jnp.int32, (1, 256), 1)

    def block(at, blocks, first):
        qr = pl.ds(pl.multiple_of(at * QUERY_ROWS, QUERY_ROWS), QUERY_ROWS)
        kr = pl.ds(pl.multiple_of(first * KEY_ROWS, KEY_ROWS), blocks * KEY_ROWS)
        query_mark = query_mark_ref[qr, :]
        key_mark = key_mark_ref[kr, :]
        for head in range(HEADS):
            low = head * head_dim
            base = low // 128 * 128
            wide = 128 if low + head_dim <= base + 128 else 256
            mine = (lane[:, :wide] >= low - base) & (lane[:, :wide] < low - base + head_dim)
            cols = slice(base, base + wide)
            queries = jnp.where(mine, q_s[qr, cols], query_mark[:, :wide])
            keys = jnp.where(mine, k_s[kr, cols], key_mark[:, :wide])
            values = jnp.where(mine, v_s[kr, cols], jnp.ones((), BF16))
            scores = lax.dot_general(queries, keys, (((1,), (1,)), ((), ())), preferred_element_type=F32)
            top = jnp.max(scores, axis=1, keepdims=True)
            probs = jnp.exp2(scores - top).astype(BF16)
            out = jnp.dot(probs, values, preferred_element_type=F32)
            spare = 0 if low > base else wide - 1
            out = (out * (1.0 / out[:, spare : spare + 1])).astype(BF16)
            if low > base:
                out = jnp.where(mine, out, context_ref[qr, cols])
            context_ref[qr, cols] = out

    def one_block(at, _):
        first = window_ref[0, at]
        blocks = window_ref[1, at]
        for size in (3, 4, 5, 6):

            @pl.when((blocks == size) if size > 3 else (blocks <= 3))
            def _():
                block(at, size, jnp.minimum(first, count // KEY_ROWS - size))

        return 0

    lax.fori_loop(0, count // QUERY_ROWS, one_block, 0)
    member = (segs_ref[...] == lax.broadcasted_iota(jnp.int32, (IMG_DEV, count), 0)).astype(F32)
    member = member.astype(BF16)
    total = jnp.sum(member.astype(F32), axis=1, keepdims=True)
    rows_sum_ref[...] = jnp.dot(member, x_ref[...], preferred_element_type=F32) / total
    context_sum_ref[...] = jnp.dot(member, context_ref[...], preferred_element_type=F32) / total


def key_windows(segs):
    blocks = segs.reshape(-1, QUERY_ROWS)
    start = jnp.sum((segs[None, :] < blocks[:, :1]).astype(jnp.int32), axis=1)
    end = jnp.sum((segs[None, :] <= blocks[:, -1:]).astype(jnp.int32), axis=1)
    first = start // KEY_ROWS
    return jnp.stack([first, (end + KEY_ROWS - 1) // KEY_ROWS - first])


def attend(x, normed, query_mark, key_mark, segs, weights):
    count, width = x.shape
    small = jax.ShapeDtypeStruct((IMG_DEV, width), F32)
    return pl.pallas_call(
        attend_kernel,
        grid=(1,),
        out_shape=(jax.ShapeDtypeStruct((count, width), BF16), small, small),
        in_specs=[VMEM] * 5 + [SMEM, pl.BlockSpec((width, 3 * width), lambda i: (0, 0), pipeline_mode=pl.Buffered(1))],
        out_specs=(VMEM,) * 3,
        scratch_shapes=[pltpu.VMEM((count, width), BF16)] * 3,
        compiler_params=BIG,
        name="attend",
    )(x, normed, query_mark, key_mark, segs.reshape(1, count), key_windows(segs), weights)


def split(values):
    high = values.astype(BF16)
    return jnp.concatenate([high, (values - high.astype(F32)).astype(BF16)], axis=0)


def join(values):
    half = values.shape[0] // 2
    return values[:half] + values[half:]


def pool_kernel(rows_mean_ref, context_mean_ref, weight_ref, unit_ref, short_ref):
    pooled = rows_mean_ref[...] + join(jnp.dot(split(context_mean_ref[...]), weight_ref[...], preferred_element_type=F32))
    unit = pooled * lax.rsqrt(jnp.sum(pooled * pooled, axis=1, keepdims=True) + 1e-06)
    unit_ref[...] = unit
    short_ref[...] = unit.astype(BF16)


def pool(rows_mean, context_mean, weights):
    images, width = rows_mean.shape
    return pl.pallas_call(
        pool_kernel,
        grid=(1,),
        out_shape=(jax.ShapeDtypeStruct((images, width), F32), jax.ShapeDtypeStruct((images, width), BF16)),
        in_specs=[VMEM] * 2 + [pl.BlockSpec((width, width), lambda i: (0, 3))],
        out_specs=(VMEM,) * 2,
        compiler_params=BIG,
        name="pool",
    )(rows_mean, context_mean, weights)


def encode_kernel(x_ref, context_ref, weight_ref, out_ref):
    attended = jnp.dot(context_ref[...], weight_ref[...], preferred_element_type=F32)
    out_ref[...] = (x_ref[...].astype(F32) + attended).astype(BF16)


def encode(x, context, weights):
    count, width = x.shape
    rows = 256
    block = pl.BlockSpec((rows, width), lambda i: (i, 0))
    return pl.pallas_call(
        encode_kernel,
        grid=(count // rows,),
        out_shape=jax.ShapeDtypeStruct((count, width), BF16),
        in_specs=[block, block, pl.BlockSpec((width, width), lambda i: (0, 3))],
        out_specs=block,
        compiler_params=BIG,
        name="encode",
    )(x, context, weights)


def sigmoid_coeffs(logits, diagonal):
    sign = jnp.where(diagonal, 1.0, -1.0).astype(F32)
    return -sign * jax.nn.sigmoid(-sign * logits)


def image_kernel(place_ref, unit_ref, text_ref, scale_ref, out_ref):
    images = unit_ref.shape[0]
    count = text_ref.shape[0]
    text = text_ref[...]
    scale = scale_ref[...]
    dots = lax.dot_general(split(unit_ref[...]), text, (((1,), (1,)), ((), ())), preferred_element_type=F32)
    logits = 10.0 * join(dots) * scale - 3.0
    own = place_ref[0] * images + lax.broadcasted_iota(jnp.int32, (images, count), 0)
    coeffs = sigmoid_coeffs(logits, own == lax.broadcasted_iota(jnp.int32, (images, count), 1))
    out_ref[...] = 10.0 * join(jnp.dot(split(coeffs * scale), text, preferred_element_type=F32))


def image_gradient(place, unit, text, scale):
    return pl.pallas_call(
        image_kernel,
        out_shape=jax.ShapeDtypeStruct(unit.shape, F32),
        in_specs=[SMEM] + [VMEM] * 3,
        out_specs=VMEM,
        compiler_params=BIG,
        name="image_gradient",
    )(place, unit, text, scale)


def text_kernel(place_ref, units_ref, text_ref, out_ref):
    images = units_ref.shape[0]
    count = text_ref.shape[0]
    text = text_ref[...].astype(F32)
    text = text * lax.rsqrt(jnp.sum(text * text, axis=1, keepdims=True) + 1e-06)
    units = units_ref[...]
    dots = lax.dot_general(split(text), units, (((1,), (1,)), ((), ())), preferred_element_type=F32)
    logits = 10.0 * join(dots) - 3.0
    image = lax.broadcasted_iota(jnp.int32, (count, images), 1) - place_ref[1] * IMG_DEV
    index = lax.broadcasted_iota(jnp.int32, (count, images), 0) - place_ref[2] * IMG_DEV
    coeffs = sigmoid_coeffs(logits, (image == index) & (image >= 0) & (image < IMG_DEV))
    out_ref[...] = 10.0 * join(jnp.dot(split(coeffs), units, preferred_element_type=F32))


def text_gradient(place, units, text):
    return pl.pallas_call(
        text_kernel,
        out_shape=jax.ShapeDtypeStruct(text.shape, F32),
        in_specs=[SMEM] + [VMEM] * 2,
        out_specs=VMEM,
        compiler_params=BIG,
        name="text_gradient",
    )(place, units, text)


def body(
    patch_rows,
    segment_ids,
    norm_gain,
    query_weight,
    key_weight,
    value_weight,
    out_weight,
    text_embeds,
):
    count, width = patch_rows.shape
    segs = segment_ids[0]
    n_row = lax.axis_size("row")
    n_col = lax.axis_size("col")
    row_at = lax.axis_index("row")
    col_at = lax.axis_index("col")
    place = jnp.stack([row_at * n_col + col_at, row_at, col_at]).astype(jnp.int32)
    depth = query_weight.shape[0]
    texts = text_embeds.shape[0]
    lanes = texts * width // depth
    packed = jnp.concatenate(
        [query_weight, key_weight, value_weight, out_weight, text_embeds.reshape(depth, lanes)], axis=1
    )
    weights = lax.all_gather(packed, "col", axis=0, tiled=True)
    row_text = weights[:, 4 * width :].reshape(n_col * texts, width)
    text = lax.all_gather(row_text, "row", axis=0, tiled=True)
    textf = text.astype(F32)
    text_scale = lax.rsqrt(jnp.sum(textf * textf, axis=1) + 1e-06).reshape(1, -1)
    normed, query_mark, key_mark = norm(patch_rows, norm_gain, segs)
    context, rows_mean, context_mean = attend(patch_rows, normed, query_mark, key_mark, segs, weights)
    unit, short = pool(rows_mean, context_mean, weights)
    units = lax.all_to_all(jnp.broadcast_to(short[None], (n_row,) + short.shape), "row", 0, 0)
    encoded = encode(patch_rows, context, weights)
    image_grad = image_gradient(place, unit, text, text_scale)
    partial = text_gradient(place, units.reshape(n_row * IMG_DEV, width), row_text)
    partial = lax.all_to_all(partial.reshape(n_col, texts, width), "col", 0, 0)
    text_grad = jnp.sum(partial, axis=0)
    return (encoded, image_grad, text_grad)


def solution(mesh):
    return jax.shard_map(
        body,
        mesh=mesh,
        in_specs=(
            P(("row", "col"), None),
            P(("row", "col"), None),
            P(),
            P("col", None),
            P("col", None),
            P("col", None),
            P("col", None),
            P(("row", "col"), None),
        ),
        out_specs=(P(("row", "col"), None), P(("row", "col"), None), P(("row", "col"), None)),
        check_vma=False,
    )
```

```python
import math

import jax
import jax.numpy as jnp
from jax import lax
from jax.experimental import pallas as pl
from jax.experimental.pallas import tpu as pltpu
from jax.sharding import PartitionSpec as P

HEADS = 16
IMG_DEV = 8
MASKED = -1e30
QUERY_ROWS = 256
KEY_ROWS = 128
SIDE = 4
AXES = ("row", "col")
F32 = jnp.float32
BF16 = jnp.bfloat16
VMEM = pl.BlockSpec(memory_space=pltpu.VMEM)
SMEM = pl.BlockSpec(memory_space=pltpu.SMEM)
ANY = pl.BlockSpec(memory_space=pl.ANY)


def whole(shape):
    return pl.BlockSpec(shape, lambda i: (0,) * len(shape), pipeline_mode=pl.Buffered(1))


def params():
    return pltpu.CompilerParams(vmem_limit_bytes=60 * 2**20)


def cost(flops, bytes_accessed):
    return pl.CostEstimate(flops=flops, bytes_accessed=bytes_accessed, transcendentals=0)


def pairs(source_of):
    def flat(x, y, z, core):
        x, y, z = x % SIDE, y % SIDE, z % SIDE
        return (x * 2 + z % 2) * 16 + y * 4 + z // 2 * 2 + core

    found = []
    for x in range(SIDE):
        for y in range(SIDE):
            for z in range(SIDE):
                for core in range(2):
                    found.append((flat(*source_of(x, y, z, core)), flat(x, y, z, core)))
    return found


FROM_CORE = pairs(lambda x, y, z, core: (x, y, z, 1 - core))
FROM_UP = pairs(lambda x, y, z, core: (x, y + 1, z, core))
FROM_DOWN = pairs(lambda x, y, z, core: (x, y - 1, z, core))
FROM_ACROSS = pairs(lambda x, y, z, core: (x, y, 3 - z, core))


def take(values, found):
    return lax.ppermute(values, AXES, found)


def pack_kernel(place_ref, q_ref, k_ref, v_ref, o_ref, text_ref, mine_ref, other_ref, rest_ref, copies_ref):
    width = q_ref.shape[1]
    half = width // 2

    def columns(at):
        cols = slice(at * half, (at + 1) * half)
        return jnp.concatenate([q_ref[:, cols], v_ref[:, cols], k_ref[:, cols]], axis=1)

    first, second = columns(0), columns(1)
    core = jnp.full(first.shape, place_ref[3], jnp.int32) == 0
    mine_ref[...] = jnp.where(core, first.astype(F32), second.astype(F32)).astype(BF16)
    other_ref[...] = jnp.where(core, second.astype(F32), first.astype(F32)).astype(BF16)
    rest_ref[:, :width] = o_ref[...]
    text = text_ref[...].astype(F32)
    blocks = [text[:, at : at + 128] for at in range(0, width, 128)]
    rest_ref[:, width:] = jnp.concatenate(blocks, axis=0).astype(BF16)
    copies_ref[...] = jnp.broadcast_to(text_ref[...][None], copies_ref.shape)


def pack(place, q, k, v, o, text, copies):
    depth, width = q.shape
    part = (depth, width // 2 * 3)
    outs = (part, part, (depth, width + 128), (copies,) + text.shape)
    return pl.pallas_call(
        pack_kernel,
        grid=(1,),
        out_shape=tuple(jax.ShapeDtypeStruct(out, BF16) for out in outs),
        in_specs=[SMEM] + [whole(values.shape) for values in (q, k, v, o, text)],
        out_specs=tuple(whole(out) for out in outs),
        compiler_params=params(),
        cost_estimate=cost(0, 2**21),
        name="pack",
    )(place, q, k, v, o, text)


def norm_kernel(x_ref, gain_ref, segs_ref, out_ref, mean_ref):
    count, width = x_ref.shape
    segs = segs_ref[...]
    marks = (segs == lax.broadcasted_iota(jnp.int32, (128, count), 0) % IMG_DEV).astype(F32)
    out_ref[:, width:] = marks.T.astype(BF16)

    def one(i, _):
        rows = pl.ds(pl.multiple_of(i * 128, 128), 128)
        xf = x_ref[rows, :].astype(F32)
        centre = xf - jnp.mean(xf, axis=1, keepdims=True)
        spread = jnp.mean(centre * centre, axis=1, keepdims=True)
        out_ref[rows, :width] = (centre * lax.rsqrt(spread + 1e-06) * gain_ref[...]).astype(BF16)
        return 0

    lax.fori_loop(0, count // 128, one, 0)
    member = marks[:IMG_DEV]
    total = jnp.sum(member, axis=1, keepdims=True)
    mean_ref[...] = jnp.dot(member.astype(BF16), x_ref[...], preferred_element_type=F32) / total


def norm(x, gain, segs):
    count, width = x.shape
    return pl.pallas_call(
        norm_kernel,
        grid=(1,),
        out_shape=(
            jax.ShapeDtypeStruct((count, width + 128), BF16),
            jax.ShapeDtypeStruct((IMG_DEV, width), F32),
        ),
        in_specs=[whole(x.shape), whole((1, width)), whole(segs.shape)],
        out_specs=(whole((count, width + 128)), whole((IMG_DEV, width))),
        compiler_params=params(),
        cost_estimate=cost(0, 2**24),
        name="norm",
    )(x, gain.reshape(1, width), segs)


def split(values):
    high = values.astype(BF16)
    return jnp.concatenate([high, (values - high.astype(F32)).astype(BF16)], axis=0)


def join(values):
    half = values.shape[0] // 2
    return values[:half] + values[half:]


def attend_kernel(place_ref, window_ref, segs_ref, normed_hbm, *refs):
    shards, (context_ref, normed_ref, weight_s, qvk_s, sems) = refs[:-5], refs[-5:]
    count = normed_ref.shape[0]
    width = weight_s.shape[0]
    half = width // 2
    head_dim = width // HEADS
    shift = half // 128 * 128

    copies = [pltpu.make_async_copy(normed_hbm, normed_ref, sems.at[len(shards)])]
    for at, shard in enumerate(shards):
        whole = min(at, 7)
        row = place_ref[4 + whole]
        if at >= 7:
            row = row + (at - 7) * shard.shape[0]
        rows = pl.ds(pl.multiple_of(row, 16), shard.shape[0])
        copies.append(pltpu.make_async_copy(shard, weight_s.at[rows, :], sems.at[at]))
    for copy in copies:
        copy.start()
    for copy in copies:
        copy.wait()

    lanes = lax.broadcasted_iota(jnp.int32, (1, 3 * half), 1)
    scale = jnp.where(lanes < half, math.log2(math.e) / math.sqrt(head_dim), 1.0).astype(F32)

    def project(i, _):
        rows = pl.ds(pl.multiple_of(i * 256, 256), 256)
        out = jnp.dot(normed_ref[rows, :width], weight_s[...], preferred_element_type=F32)
        qvk_s[rows, : 3 * half] = (out * scale).astype(BF16)
        return 0

    lax.fori_loop(0, count // 256, project, 0)
    lane = lax.broadcasted_iota(jnp.int32, (1, 256), 1)

    def span(low):
        base = low // 128 * 128
        wide = 128 if low + head_dim <= base + 128 else 256
        mine = (lane[:, :wide] >= low - base) & (lane[:, :wide] < low - base + head_dim)
        return base, wide, mine

    def block(at, blocks, first):
        qr = pl.ds(pl.multiple_of(at * QUERY_ROWS, QUERY_ROWS), QUERY_ROWS)
        kr = pl.ds(pl.multiple_of(first * KEY_ROWS, KEY_ROWS), blocks * KEY_ROWS)
        query_mark = normed_ref[qr, width:]
        query_mark = jnp.concatenate([query_mark, query_mark], axis=1)
        key_mark = ((normed_ref[kr, width:].astype(F32) - 1.0) * -MASKED).astype(BF16)
        key_mark = jnp.concatenate([key_mark, key_mark], axis=1)
        for head in range(HEADS // 2):
            base, wide, mine = span(head * head_dim)
            queries = jnp.where(mine, qvk_s[qr, base : base + wide], query_mark[:, :wide])
            base += 2 * half
            keys = jnp.where(mine, qvk_s[kr, base : base + wide], key_mark[:, :wide])
            low = half + head * head_dim
            base, wide, mine = span(low)
            values = jnp.where(mine, qvk_s[kr, base : base + wide], jnp.ones((), BF16))
            scores = lax.dot_general(queries, keys, (((1,), (1,)), ((), ())), preferred_element_type=F32)
            top = jnp.max(scores, axis=1, keepdims=True)
            probs = jnp.exp2(scores - top).astype(BF16)
            out = jnp.dot(probs, values, preferred_element_type=F32)
            spare = 0 if low > base else wide - 1
            out = (out * (1.0 / out[:, spare : spare + 1])).astype(BF16)
            cols = slice(base - shift, base - shift + wide)
            old = jnp.zeros((), BF16) if head == 0 else context_ref[qr, cols]
            context_ref[qr, cols] = jnp.where(mine, out, old)

    def one_block(at, _):
        first = window_ref[0, at]
        blocks = window_ref[1, at]
        for size in (3, 4, 5, 6):

            @pl.when((blocks == size) if size > 3 else (blocks <= 3))
            def _():
                block(at, size, jnp.minimum(first, count // KEY_ROWS - size))

        return 0

    lax.fori_loop(0, count // QUERY_ROWS, one_block, 0)
    member = (segs_ref[...] == lax.broadcasted_iota(jnp.int32, (IMG_DEV, count), 0)).astype(F32)
    total = jnp.sum(member, axis=1, keepdims=True)
    sums = jnp.dot(member.astype(BF16), context_ref[:count, :], preferred_element_type=F32)
    context_ref[count:, :] = split(sums / total)


def key_windows(segs):
    blocks = segs.reshape(-1, QUERY_ROWS)
    start = jnp.sum((segs < blocks[:, :1]).astype(jnp.int32), axis=1)
    end = jnp.sum((segs <= blocks[:, -1:]).astype(jnp.int32), axis=1)
    first = start // KEY_ROWS
    return jnp.stack([first, (end + KEY_ROWS - 1) // KEY_ROWS - first])


def attend(place, segs, normed, shards):
    count = normed.shape[0]
    width = normed.shape[1] - 128
    columns = width // 2 * 3
    across = width // 2 + 64
    return pl.pallas_call(
        attend_kernel,
        grid=(1,),
        out_shape=jax.ShapeDtypeStruct((count + 2 * IMG_DEV, across), BF16),
        in_specs=[SMEM] * 2 + [whole(segs.shape)] + [ANY] * (len(shards) + 1),
        out_specs=whole((count + 2 * IMG_DEV, across)),
        scratch_shapes=[
            pltpu.VMEM(normed.shape, BF16),
            pltpu.VMEM((width, columns), BF16),
            pltpu.VMEM((count, columns + 64), BF16),
            pltpu.SemaphoreType.DMA((len(shards) + 1,)),
        ],
        compiler_params=params(),
        cost_estimate=cost(10**10, 2**24),
        name="attend",
    )(place, key_windows(segs), segs, normed, *shards)


def both_halves(place_ref, own, other):
    first = jnp.full(own.shape, place_ref[3], jnp.int32) == 0
    own, other = own.astype(F32), other.astype(F32)
    halves = [jnp.where(first, own, other), jnp.where(first, other, own)]
    return jnp.concatenate([part[:, 64:] for part in halves], axis=1).astype(BF16)


def pool_kernel(place_ref, rows_mean_ref, own_ref, other_ref, weight_ref, unit_ref, out_ref):
    context = both_halves(place_ref, own_ref[...], other_ref[...])
    pooled = rows_mean_ref[...] + join(jnp.dot(context, weight_ref[...], preferred_element_type=F32))
    unit = pooled * lax.rsqrt(jnp.sum(pooled * pooled, axis=1, keepdims=True) + 1e-06)
    unit_ref[...] = unit
    out_ref[...] = jnp.broadcast_to(unit.astype(BF16)[None], out_ref.shape)


def pool(place, rows_mean, own, other, rest, copies):
    images, width = rows_mean.shape
    last = own.shape[0] // (2 * images) - 1
    tail = pl.BlockSpec((2 * images, own.shape[1]), lambda i: (last, 0))
    return pl.pallas_call(
        pool_kernel,
        grid=(1,),
        out_shape=(jax.ShapeDtypeStruct((images, width), F32), jax.ShapeDtypeStruct((copies, images, width), BF16)),
        in_specs=[SMEM, whole((images, width)), tail, tail, whole((width, width))],
        out_specs=(whole((images, width)), whole((copies, images, width))),
        compiler_params=params(),
        cost_estimate=cost(2**25, 2**22),
        name="pool",
    )(place, rows_mean, own, other, rest)


def encode_kernel(place_ref, x_ref, own_ref, other_ref, weight_ref, out_ref):
    context = both_halves(place_ref, own_ref[...], other_ref[...])
    attended = jnp.dot(context, weight_ref[...], preferred_element_type=F32)
    out_ref[...] = (x_ref[...].astype(F32) + attended).astype(BF16)


def encode(place, x, own, other, rest):
    count, width = x.shape
    rows = 256
    block = pl.BlockSpec((rows, width), lambda i: (i, 0))
    half = pl.BlockSpec((rows, own.shape[1]), lambda i: (i, 0))
    return pl.pallas_call(
        encode_kernel,
        grid=(count // rows,),
        out_shape=jax.ShapeDtypeStruct((count, width), BF16),
        in_specs=[SMEM, block, half, half, pl.BlockSpec((width, width), lambda i: (0, 0))],
        out_specs=block,
        compiler_params=params(),
        cost_estimate=cost(3 * 10**9, 2**24),
        name="encode",
    )(place, x, own, other, rest)


def text_rows(packed, width):
    columns = width // 128
    texts = packed.shape[0] // columns
    packed = packed.astype(F32).reshape(texts // 8, columns * 8, 128)
    pieces = [packed[:, at * 8 : at * 8 + 8, :].reshape(texts, 128) for at in range(columns)]
    return jnp.concatenate(pieces, axis=1)


def inverse_norm(values):
    return lax.rsqrt(jnp.sum(values * values, axis=1, keepdims=True) + 1e-06)


def sigmoid_coeffs(logits, diagonal):
    sign = jnp.where(diagonal, 1.0, -1.0).astype(F32)
    return -10.0 * sign * jax.nn.sigmoid(-sign * logits)


def text_kernel(place_ref, units_ref, text_ref, out_ref):
    units = units_ref[...]
    images, width = units.shape
    text = text_rows(text_ref[...], width)
    texts = text.shape[0]
    scale = inverse_norm(text)
    dots = lax.dot_general(text.astype(BF16), units, (((1,), (1,)), ((), ())), preferred_element_type=F32)
    image = lax.broadcasted_iota(jnp.int32, (texts, images), 1) - place_ref[1] * IMG_DEV
    index = lax.broadcasted_iota(jnp.int32, (texts, images), 0) - place_ref[2] * IMG_DEV
    diagonal = (image == index) & (image >= 0) & (image < IMG_DEV)
    coeffs = sigmoid_coeffs(10.0 * dots * scale - 3.0, diagonal)
    out_ref[...] = join(jnp.dot(split(coeffs), units, preferred_element_type=F32)).astype(BF16)


def text_terms(place, units, rest):
    images, width = units.shape
    texts = rest.shape[0] * 128 // width
    return pl.pallas_call(
        text_kernel,
        grid=(1,),
        out_shape=jax.ShapeDtypeStruct((texts, width), BF16),
        in_specs=[SMEM, whole((images, width)), pl.BlockSpec((rest.shape[0], 128), lambda i: (0, width // 128))],
        out_specs=whole((texts, width)),
        compiler_params=params(),
        cost_estimate=cost(2**26, 2**21),
        name="text_terms",
    )(place, units, rest)


def image_kernel(place_ref, unit_ref, text_ref, out_ref):
    unit = unit_ref[...]
    images, width = unit.shape
    text = text_ref[...]
    texts = text.shape[0]
    scale = inverse_norm(text.astype(F32))
    dots = lax.dot_general(text, split(unit), (((1,), (1,)), ((), ())), preferred_element_type=F32)
    dots = dots[:, :images] + dots[:, images:]
    image = lax.broadcasted_iota(jnp.int32, (texts, images), 1) + place_ref[0] * images
    diagonal = image == lax.broadcasted_iota(jnp.int32, (texts, images), 0)
    coeffs = sigmoid_coeffs(10.0 * dots * scale - 3.0, diagonal) * scale
    out_ref[...] = join(jnp.dot(split(coeffs.T), text, preferred_element_type=F32))


def image_gradient(place, unit, text):
    return pl.pallas_call(
        image_kernel,
        grid=(1,),
        out_shape=jax.ShapeDtypeStruct(unit.shape, F32),
        in_specs=[SMEM, whole(unit.shape), whole(text.shape)],
        out_specs=whole(unit.shape),
        compiler_params=params(),
        cost_estimate=cost(2**28, 2**22),
        name="image_gradient",
    )(place, unit, text)


def gather_weights(own, beside):
    up, down, across, beside = lax.optimization_barrier(
        (take(own, FROM_UP), take(own, FROM_DOWN), take(own, FROM_ACROSS), beside)
    )
    far, across_up, across_down = lax.optimization_barrier(
        (take(up, FROM_UP), take(up, FROM_ACROSS), take(across, FROM_DOWN))
    )
    third = own.shape[0] // 3
    last = [
        take(far[:third], FROM_ACROSS),
        take(across_up[third : 2 * third], FROM_UP),
        take(across_down[2 * third :], FROM_DOWN),
    ]
    return [own, up, down, far, across, across_up, across_down] + last, beside


def body(
    patch_rows,
    segment_ids,
    norm_gain,
    query_weight,
    key_weight,
    value_weight,
    out_weight,
    text_embeds,
):
    count, width = patch_rows.shape
    n_row = lax.axis_size("row")
    n_col = lax.axis_size("col")
    row_at = lax.axis_index("row")
    col_at = lax.axis_index("col")
    core = col_at % 2
    y_at = col_at // 4
    z_hi = col_at // 2 % 2
    depth = query_weight.shape[0] * 2
    steps = [(0, 0), (1, 0), (-1, 0), (2, 0), (0, 1), (1, 1), (-1, 1), (2, 1)]
    firsts = [((y_at + dy) % SIDE * 2 + (z_hi + dz) % 2) * depth for dy, dz in steps]
    place = jnp.stack([col_at * n_row + row_at, row_at, col_at, core] + firsts).astype(jnp.int32)
    texts = text_embeds.shape[0]

    mine, other, rest, copies = pack(place, query_weight, key_weight, value_weight, out_weight, text_embeds, n_row)
    rest = lax.all_gather(rest, "col", axis=0, tiled=True)
    theirs = take(other, FROM_CORE)
    other_segs = take(segment_ids, FROM_CORE)
    own = jnp.where(core == 0, jnp.concatenate([mine, theirs]), jnp.concatenate([theirs, mine]))
    own, rows, other_segs, copies = lax.optimization_barrier((own, patch_rows, other_segs, copies))
    normed, rows_mean = norm(rows, norm_gain, segment_ids)
    column_text = lax.all_to_all(copies, "row", 0, 0)
    shards, (normed, column_text) = gather_weights(own, (normed, column_text))
    every_text = lax.all_gather(column_text.reshape(n_row * texts, width), "col", axis=0, tiled=True)
    other_normed = take(normed, FROM_CORE)
    for_other = attend(place, other_segs, other_normed, shards)
    context_other = take(for_other, FROM_CORE)
    context_own = attend(place, segment_ids, normed, shards)
    context_own, rest = lax.optimization_barrier((context_own, rest))
    unit, units = pool(place, rows_mean, context_own, context_other, rest, n_row)
    units = lax.all_to_all(units, "row", 0, 0)
    encoded = encode(place, patch_rows, context_own, context_other, rest)
    units, encoded = lax.optimization_barrier((units, encoded))
    terms = text_terms(place, units.reshape(n_row * IMG_DEV, width), rest)
    terms, unit, every_text = lax.optimization_barrier((terms, unit, every_text))
    terms = lax.all_to_all(terms.reshape(n_col, texts, width), "col", 0, 0)
    image_grad = image_gradient(place, unit, every_text)
    return (encoded, image_grad, jnp.sum(terms.astype(F32), axis=0))


def solution(mesh):
    return jax.shard_map(
        body,
        mesh=mesh,
        in_specs=(
            P(("row", "col"), None),
            P(("row", "col"), None),
            P(),
            P("col", None),
            P("col", None),
            P("col", None),
            P("col", None),
            P(("row", "col"), None),
        ),
        out_specs=(P(("row", "col"), None), P(("row", "col"), None), P(("row", "col"), None)),
        check_vma=False,
    )
```

```python
import math

import jax
import jax.numpy as jnp
from jax import lax
from jax.experimental import pallas as pl
from jax.experimental.pallas import tpu as pltpu
from jax.sharding import PartitionSpec as P

HEADS = 16
IMG_DEV = 8
MASKED = -1e30
QUERY_ROWS = 256
KEY_ROWS = 128
PROJECT_CHUNKS = 4
SIDE = 4
AXES = ("row", "col")
F32 = jnp.float32
BF16 = jnp.bfloat16
VMEM = pl.BlockSpec(memory_space=pltpu.VMEM)
SMEM = pl.BlockSpec(memory_space=pltpu.SMEM)
ANY = pl.BlockSpec(memory_space=pl.ANY)


def whole(shape):
    return pl.BlockSpec(shape, lambda i: (0,) * len(shape), pipeline_mode=pl.Buffered(1))


def params():
    return pltpu.CompilerParams(vmem_limit_bytes=60 * 2**20)


def cost(flops, bytes_accessed):
    return pl.CostEstimate(flops=flops, bytes_accessed=bytes_accessed, transcendentals=0)


def pairs(source_of):
    def flat(x, y, z, core):
        x, y, z = x % SIDE, y % SIDE, z % SIDE
        return (x * 2 + z % 2) * 16 + y * 4 + z // 2 * 2 + core

    found = []
    for x in range(SIDE):
        for y in range(SIDE):
            for z in range(SIDE):
                for core in range(2):
                    found.append((flat(*source_of(x, y, z, core)), flat(x, y, z, core)))
    return found


SAME_CORE = [list(range(core, 16, 2)) for core in range(2)]
FROM_CORE = pairs(lambda x, y, z, core: (x, y, z, 1 - core))
FROM_UP = pairs(lambda x, y, z, core: (x, y + 1, z, core))
FROM_DOWN = pairs(lambda x, y, z, core: (x, y - 1, z, core))
FROM_ACROSS = pairs(lambda x, y, z, core: (x, y, 3 - z, core))


def take(values, found):
    return lax.ppermute(values, AXES, found)


def pack_kernel(place_ref, q_ref, k_ref, v_ref, mine_ref, other_ref):
    width = q_ref.shape[1]
    head_dim = width // HEADS

    def columns(core):
        cols = [slice(head * head_dim, (head + 1) * head_dim) for head in range(core, HEADS, 2)]
        return jnp.concatenate([ref[:, col] for ref in (q_ref, v_ref, k_ref) for col in cols], axis=1)

    first, second = columns(0), columns(1)
    core = jnp.full(first.shape, place_ref[3], jnp.int32) == 0
    mine_ref[...] = jnp.where(core, first.astype(F32), second.astype(F32)).astype(BF16)
    other_ref[...] = jnp.where(core, second.astype(F32), first.astype(F32)).astype(BF16)


def pack(place, q, k, v):
    depth, width = q.shape
    part = (depth, width // 2 * 3)
    return pl.pallas_call(
        pack_kernel,
        grid=(1,),
        out_shape=(jax.ShapeDtypeStruct(part, BF16),) * 2,
        in_specs=[SMEM] + [whole(q.shape)] * 3,
        out_specs=(whole(part),) * 2,
        compiler_params=params(),
        cost_estimate=cost(0, 2**21),
        name="pack",
    )(place, q, k, v)


def copies_kernel(in_ref, out_ref):
    out_ref[...] = jnp.broadcast_to(in_ref[...][None], out_ref.shape)


def copies_of(values, copies):
    out = (copies,) + values.shape
    return pl.pallas_call(
        copies_kernel,
        grid=(1,),
        out_shape=jax.ShapeDtypeStruct(out, BF16),
        in_specs=[whole(values.shape)],
        out_specs=whole(out),
        compiler_params=params(),
        cost_estimate=cost(0, 2**22),
        name="copies",
    )(values)


def norm_kernel(x_ref, gain_ref, segs_ref, out_ref, mean_ref):
    count, width = x_ref.shape
    segs = segs_ref[...]
    marks = (segs == lax.broadcasted_iota(jnp.int32, (128, count), 0) % IMG_DEV).astype(F32)
    out_ref[:, width:] = marks.T.astype(BF16)

    def one(i, _):
        rows = pl.ds(pl.multiple_of(i * 128, 128), 128)
        xf = x_ref[rows, :].astype(F32)
        centre = xf - jnp.mean(xf, axis=1, keepdims=True)
        spread = jnp.mean(centre * centre, axis=1, keepdims=True)
        out_ref[rows, :width] = (centre * lax.rsqrt(spread + 1e-06) * gain_ref[...]).astype(BF16)
        return 0

    lax.fori_loop(0, count // 128, one, 0)
    member = marks[:IMG_DEV]
    total = jnp.sum(member, axis=1, keepdims=True)
    mean_ref[...] = jnp.dot(member.astype(BF16), x_ref[...], preferred_element_type=F32) / total


def norm(x, gain, segs):
    count, width = x.shape
    return pl.pallas_call(
        norm_kernel,
        grid=(1,),
        out_shape=(
            jax.ShapeDtypeStruct((count, width + 128), BF16),
            jax.ShapeDtypeStruct((IMG_DEV, width), F32),
        ),
        in_specs=[whole(x.shape), whole((1, width)), whole(segs.shape)],
        out_specs=(whole((count, width + 128)), whole((IMG_DEV, width))),
        compiler_params=params(),
        cost_estimate=cost(0, 2**24),
        name="norm",
    )(x, gain.reshape(1, width), segs)


def split(values):
    high = values.astype(BF16)
    return jnp.concatenate([high, (values - high.astype(F32)).astype(BF16)], axis=0)


def join(values):
    half = values.shape[0] // 2
    return values[:half] + values[half:]


def attend_kernel(place_ref, window_ref, segs_ref, normed_hbm, *refs):
    shards, (context_ref, normed_ref, weight_s, qvk_s, sems) = refs[:-5], refs[-5:]
    count = normed_ref.shape[0]
    width = weight_s.shape[0]
    half = width // 2
    head_dim = width // HEADS
    shift = half // 128 * 128

    chunk = count // PROJECT_CHUNKS

    copies = []
    for at, shard in enumerate(shards):
        whole = min(at, 7)
        row = place_ref[4 + whole]
        if at >= 7:
            row = row + (at - 7) * shard.shape[0]
        rows = pl.ds(pl.multiple_of(row, 16), shard.shape[0])
        copies.append(pltpu.make_async_copy(shard, weight_s.at[rows, :], sems.at[at]))
    for copy in copies:
        copy.start()

    def normed_copy(i):
        rows = pl.ds(pl.multiple_of(i * chunk, chunk), chunk)
        return pltpu.make_async_copy(normed_hbm.at[rows, :], normed_ref.at[rows, :], sems.at[len(shards) + i])

    for i in range(PROJECT_CHUNKS):
        normed_copy(i).start()
    for copy in copies:
        copy.wait()

    lanes = lax.broadcasted_iota(jnp.int32, (1, 3 * half), 1)
    scale = jnp.where(lanes < half, math.log2(math.e) / math.sqrt(head_dim), 1.0).astype(F32)

    def project(i, _):
        normed_copy(i).wait()
        rows = pl.ds(pl.multiple_of(i * chunk, chunk), chunk)
        out = jnp.dot(normed_ref[rows, :width], weight_s[...], preferred_element_type=F32)
        qvk_s[rows, : 3 * half] = (out * scale).astype(BF16)
        return 0

    lax.fori_loop(0, PROJECT_CHUNKS, project, 0)
    lane = lax.broadcasted_iota(jnp.int32, (1, 256), 1)

    def span(low):
        base = low // 128 * 128
        wide = 128 if low + head_dim <= base + 128 else 256
        mine = (lane[:, :wide] >= low - base) & (lane[:, :wide] < low - base + head_dim)
        return base, wide, mine

    def block(at, blocks, first):
        qr = pl.ds(pl.multiple_of(at * QUERY_ROWS, QUERY_ROWS), QUERY_ROWS)
        kr = pl.ds(pl.multiple_of(first * KEY_ROWS, KEY_ROWS), blocks * KEY_ROWS)
        query_mark = normed_ref[qr, width:]
        query_mark = jnp.concatenate([query_mark, query_mark], axis=1)
        key_mark = ((normed_ref[kr, width:].astype(F32) - 1.0) * -MASKED).astype(BF16)
        key_mark = jnp.concatenate([key_mark, key_mark], axis=1)
        for head in range(HEADS // 2):
            base, wide, mine = span(head * head_dim)
            queries = jnp.where(mine, qvk_s[qr, base : base + wide], query_mark[:, :wide])
            base += 2 * half
            keys = jnp.where(mine, qvk_s[kr, base : base + wide], key_mark[:, :wide])
            low = half + head * head_dim
            base, wide, mine = span(low)
            values = jnp.where(mine, qvk_s[kr, base : base + wide], jnp.ones((), BF16))
            scores = lax.dot_general(queries, keys, (((1,), (1,)), ((), ())), preferred_element_type=F32)
            top = jnp.max(scores, axis=1, keepdims=True)
            probs = jnp.exp2(scores - top).astype(BF16)
            out = jnp.dot(probs, values, preferred_element_type=F32)
            spare = 0 if low > base else wide - 1
            out = (out * (1.0 / out[:, spare : spare + 1])).astype(BF16)
            cols = slice(base - shift, base - shift + wide)
            old = jnp.zeros((), BF16) if head == 0 else context_ref[qr, cols]
            context_ref[qr, cols] = jnp.where(mine, out, old)

    def one_block(at, _):
        first = window_ref[0, at]
        blocks = window_ref[1, at]
        for size in (3, 4, 5, 6):

            @pl.when((blocks == size) if size > 3 else (blocks <= 3))
            def _():
                block(at, size, jnp.minimum(first, count // KEY_ROWS - size))

        return 0

    lax.fori_loop(0, count // QUERY_ROWS, one_block, 0)
    member = (segs_ref[...] == lax.broadcasted_iota(jnp.int32, (IMG_DEV, count), 0)).astype(F32)
    total = jnp.sum(member, axis=1, keepdims=True)
    sums = jnp.dot(member.astype(BF16), context_ref[:count, :], preferred_element_type=F32)
    context_ref[count:, :] = split(sums / total)


def key_windows(segs):
    blocks = segs.reshape(-1, QUERY_ROWS)
    start = jnp.sum((segs < blocks[:, :1]).astype(jnp.int32), axis=1)
    end = jnp.sum((segs <= blocks[:, -1:]).astype(jnp.int32), axis=1)
    first = start // KEY_ROWS
    return jnp.stack([first, (end + KEY_ROWS - 1) // KEY_ROWS - first])


def attend(place, segs, normed, shards):
    count = normed.shape[0]
    width = normed.shape[1] - 128
    columns = width // 2 * 3
    across = width // 2 + 64
    return pl.pallas_call(
        attend_kernel,
        grid=(1,),
        out_shape=jax.ShapeDtypeStruct((count + 2 * IMG_DEV, across), BF16),
        in_specs=[SMEM] * 2 + [whole(segs.shape)] + [ANY] * (len(shards) + 1),
        out_specs=whole((count + 2 * IMG_DEV, across)),
        scratch_shapes=[
            pltpu.VMEM(normed.shape, BF16),
            pltpu.VMEM((width, columns), BF16),
            pltpu.VMEM((count, columns + 64), BF16),
            pltpu.SemaphoreType.DMA((len(shards) + PROJECT_CHUNKS,)),
        ],
        compiler_params=params(),
        cost_estimate=cost(10**10, 2**24),
        name="attend",
    )(place, key_windows(segs), segs, normed, *shards)


def pool_kernel(rows_mean_ref, own_ref, other_ref, own_weight_ref, other_weight_ref, unit_ref, out_ref):
    pooled = rows_mean_ref[...]
    for context_ref, weight_ref in ((own_ref, own_weight_ref), (other_ref, other_weight_ref)):
        pooled += join(jnp.dot(context_ref[:, 64:], weight_ref[...], preferred_element_type=F32))
    unit = pooled * lax.rsqrt(jnp.sum(pooled * pooled, axis=1, keepdims=True) + 1e-06)
    unit_ref[...] = unit
    out_ref[...] = jnp.broadcast_to(unit.astype(BF16)[None], out_ref.shape)


def pool(rows_mean, own, other, own_weight, other_weight, copies):
    images, width = rows_mean.shape
    last = own.shape[0] // (2 * images) - 1
    tail = pl.BlockSpec((2 * images, own.shape[1]), lambda i: (last, 0))
    weight = whole(own_weight.shape)
    return pl.pallas_call(
        pool_kernel,
        grid=(1,),
        out_shape=(jax.ShapeDtypeStruct((images, width), F32), jax.ShapeDtypeStruct((copies, images, width), BF16)),
        in_specs=[whole((images, width)), tail, tail, weight, weight],
        out_specs=(whole((images, width)), whole((copies, images, width))),
        compiler_params=params(),
        cost_estimate=cost(2**25, 2**22),
        name="pool",
    )(rows_mean, own, other, own_weight, other_weight)


def encode_kernel(x_ref, own_ref, other_ref, own_weight_ref, other_weight_ref, out_ref, weight_s):
    depth = own_weight_ref.shape[0] + 64

    @pl.when(pl.program_id(0) == 0)
    def _():
        for at, weight_ref in enumerate((own_weight_ref, other_weight_ref)):
            weight_s[at * depth : at * depth + 64, :] = jnp.zeros((64, weight_s.shape[1]), BF16)
            weight_s[at * depth + 64 : (at + 1) * depth, :] = weight_ref[...]

    attended = jnp.dot(own_ref[...], weight_s[:depth, :], preferred_element_type=F32)
    attended += jnp.dot(other_ref[...], weight_s[depth:, :], preferred_element_type=F32)
    out_ref[...] = (x_ref[...].astype(F32) + attended).astype(BF16)


def encode(x, own, other, own_weight, other_weight):
    count, width = x.shape
    rows = 512
    block = pl.BlockSpec((rows, width), lambda i: (i, 0))
    half = pl.BlockSpec((rows, own.shape[1]), lambda i: (i, 0))
    weight = whole(own_weight.shape)
    return pl.pallas_call(
        encode_kernel,
        grid=(count // rows,),
        out_shape=jax.ShapeDtypeStruct((count, width), BF16),
        in_specs=[block, half, half, weight, weight],
        out_specs=block,
        scratch_shapes=[pltpu.VMEM((2 * own.shape[1], width), BF16)],
        compiler_params=params(),
        cost_estimate=cost(3 * 10**9, 2**24),
        name="encode",
    )(x, own, other, own_weight, other_weight)


def inverse_norm(values):
    return lax.rsqrt(jnp.sum(values * values, axis=1, keepdims=True) + 1e-06)


def sigmoid_coeffs(logits, diagonal):
    sign = jnp.where(diagonal, 1.0, -1.0).astype(F32)
    return -10.0 * sign * jax.nn.sigmoid(-sign * logits)


def text_kernel(place_ref, units_ref, mine_ref, theirs_ref, out_ref):
    units = units_ref[...]
    images, width = units.shape
    owners = mine_ref.shape[0]
    texts = owners * IMG_DEV
    row, core = place_ref[1], place_ref[3]
    for text_ref, at in ((mine_ref, core), (theirs_ref, 1 - core)):
        text = text_ref[:, row].astype(F32).reshape(texts, width)
        scale = inverse_norm(text)
        dots = lax.dot_general(text.astype(BF16), units, (((1,), (1,)), ((), ())), preferred_element_type=F32)
        image = lax.broadcasted_iota(jnp.int32, (texts, images), 1) - row * IMG_DEV
        index = lax.broadcasted_iota(jnp.int32, (texts, images), 0)
        index = index // IMG_DEV * 2 * IMG_DEV + index % IMG_DEV + (at - place_ref[2]) * IMG_DEV
        diagonal = (image == index) & (image >= 0) & (image < IMG_DEV)
        coeffs = sigmoid_coeffs(10.0 * dots * scale - 3.0, diagonal)
        term = join(jnp.dot(split(coeffs), units, preferred_element_type=F32))
        out_ref[:, at] = term.reshape(owners, IMG_DEV, width).astype(BF16)


def text_terms(place, units, mine, theirs):
    images, width = units.shape
    out = (mine.shape[0], 2, IMG_DEV, width)
    return pl.pallas_call(
        text_kernel,
        grid=(1,),
        out_shape=jax.ShapeDtypeStruct(out, BF16),
        in_specs=[SMEM, whole((images, width)), whole(mine.shape), whole(mine.shape)],
        out_specs=whole(out),
        compiler_params=params(),
        cost_estimate=cost(2**26, 2**21),
        name="text_terms",
    )(place, units, mine, theirs)


def image_kernel(place_ref, unit_ref, mine_ref, theirs_ref, out_ref):
    unit = unit_ref[...]
    images, width = unit.shape
    grad = jnp.zeros(unit.shape, F32)
    for text_ref, low in ((mine_ref, place_ref[0]), (theirs_ref, -1)):
        text = text_ref[...]
        texts = text.shape[0]
        scale = inverse_norm(text.astype(F32))
        dots = lax.dot_general(text, split(unit), (((1,), (1,)), ((), ())), preferred_element_type=F32)
        dots = dots[:, :images] + dots[:, images:]
        image = lax.broadcasted_iota(jnp.int32, (texts, images), 1) + low * images
        diagonal = image == lax.broadcasted_iota(jnp.int32, (texts, images), 0)
        coeffs = sigmoid_coeffs(10.0 * dots * scale - 3.0, diagonal) * scale
        grad += join(jnp.dot(split(coeffs.T), text, preferred_element_type=F32))
    out_ref[...] = grad


def image_gradient(place, unit, mine, theirs):
    return pl.pallas_call(
        image_kernel,
        grid=(1,),
        out_shape=jax.ShapeDtypeStruct(unit.shape, F32),
        in_specs=[SMEM, whole(unit.shape), whole(mine.shape), whole(mine.shape)],
        out_specs=whole(unit.shape),
        compiler_params=params(),
        cost_estimate=cost(2**28, 2**22),
        name="image_gradient",
    )(place, unit, mine, theirs)


def gather_weights(own, first, second):
    up, down, across, beside = lax.optimization_barrier(
        (take(own, FROM_UP), take(own, FROM_DOWN), take(own, FROM_ACROSS), first())
    )
    far, across_up, across_down, beside = lax.optimization_barrier(
        (take(up, FROM_UP), take(up, FROM_ACROSS), take(across, FROM_DOWN), second(beside))
    )
    third = own.shape[0] // 3
    last = [
        take(far[:third], FROM_ACROSS),
        take(across_up[third : 2 * third], FROM_UP),
        take(across_down[2 * third :], FROM_DOWN),
    ]
    return [own, up, down, far, across, across_up, across_down] + last, beside


def body(
    patch_rows,
    segment_ids,
    norm_gain,
    query_weight,
    key_weight,
    value_weight,
    out_weight,
    text_embeds,
):
    count, width = patch_rows.shape
    n_row = lax.axis_size("row")
    n_col = lax.axis_size("col")
    row_at = lax.axis_index("row")
    col_at = lax.axis_index("col")
    core = col_at % 2
    y_at = col_at // 4
    z_hi = col_at // 2 % 2
    depth = query_weight.shape[0] * 2
    steps = [(0, 0), (1, 0), (-1, 0), (2, 0), (0, 1), (1, 1), (-1, 1), (2, 1)]
    firsts = [((y_at + dy) % SIDE * 2 + (z_hi + dz) % 2) * depth for dy, dz in steps]
    place = jnp.stack([col_at // 2 * n_row + row_at, row_at, col_at, core] + firsts).astype(jnp.int32)
    texts = text_embeds.shape[0]

    owners = n_col // 2
    mine, other = pack(place, query_weight, key_weight, value_weight)
    theirs = take(other, FROM_CORE)
    other_segs = take(segment_ids, FROM_CORE)
    own = jnp.where(core == 0, jnp.concatenate([mine, theirs]), jnp.concatenate([theirs, mine]))
    own, rows, other_segs, out_rows, own_text = lax.optimization_barrier(
        (own, patch_rows, other_segs, out_weight, text_embeds)
    )

    def first():
        column_text = lax.all_to_all(copies_of(own_text, n_row), "row", 0, 0)
        return norm(rows, norm_gain, segment_ids), column_text

    def second(beside):
        (normed, rows_mean), column_text = beside
        text_copies = copies_of(column_text.reshape(n_row * texts, width), owners)
        return normed, take(normed, FROM_CORE), rows_mean, text_copies, copies_of(out_rows, owners)

    shards, beside = gather_weights(own, first, second)
    normed, other_normed, rows_mean, text_copies, out_copies = beside
    own_out = lax.all_to_all(out_copies, "col", 0, 0, axis_index_groups=SAME_CORE)
    for_other = attend(place, other_segs, other_normed, shards)
    for_other, own_out = lax.optimization_barrier((for_other, own_out))
    context_other = take(for_other, FROM_CORE)
    own_out = own_out.reshape(width // 2, width)
    other_out = take(own_out, FROM_CORE)
    own_text = lax.all_to_all(text_copies, "col", 0, 0, axis_index_groups=SAME_CORE)
    own_text = own_text.reshape(owners, n_row, texts, width)
    context_own = attend(place, segment_ids, normed, shards)
    unit, units = pool(rows_mean, context_own, context_other, own_out, other_out, n_row)
    units, own_text = lax.optimization_barrier((units, own_text))
    other_text = take(own_text, FROM_CORE)
    units = lax.all_to_all(units, "row", 0, 0)
    encoded = encode(patch_rows, context_own, context_other, own_out, other_out)
    units, encoded = lax.optimization_barrier((units, encoded))
    terms = text_terms(place, units.reshape(n_row * IMG_DEV, width), own_text, other_text)
    terms, unit = lax.optimization_barrier((terms, unit))
    terms = lax.all_to_all(terms.reshape(n_col, texts, width), "col", 0, 0)
    every = owners * n_row * texts
    image_grad = image_gradient(place, unit, own_text.reshape(every, width), other_text.reshape(every, width))
    return (encoded, image_grad, jnp.sum(terms.astype(F32), axis=0))


def solution(mesh):
    return jax.shard_map(
        body,
        mesh=mesh,
        in_specs=(
            P(("row", "col"), None),
            P(("row", "col"), None),
            P(),
            P("col", None),
            P("col", None),
            P("col", None),
            P("col", None),
            P(("row", "col"), None),
        ),
        out_specs=(P(("row", "col"), None), P(("row", "col"), None), P(("row", "col"), None)),
        check_vma=False,
    )
```

```python
import math

import jax
import jax.numpy as jnp
from jax import lax
from jax.experimental import pallas as pl
from jax.experimental.pallas import tpu as pltpu
from jax.sharding import PartitionSpec as P

HEADS = 16
IMG_DEV = 8
MASKED = -1e30
QUERY_ROWS = 256
KEY_ROWS = 128
PROJECT_CHUNKS = 4
SIDE = 4
AXES = ("row", "col")
F32 = jnp.float32
BF16 = jnp.bfloat16
VMEM = pl.BlockSpec(memory_space=pltpu.VMEM)
SMEM = pl.BlockSpec(memory_space=pltpu.SMEM)
ANY = pl.BlockSpec(memory_space=pl.ANY)


def whole(shape):
    return pl.BlockSpec(shape, lambda i: (0,) * len(shape), pipeline_mode=pl.Buffered(1))


def params(mebibytes=60):
    return pltpu.CompilerParams(vmem_limit_bytes=mebibytes * 2**20)


def cost(flops, bytes_accessed):
    return pl.CostEstimate(flops=flops, bytes_accessed=bytes_accessed, transcendentals=0)


def pairs(source_of):
    def flat(x, y, z, core):
        x, y, z = x % SIDE, y % SIDE, z % SIDE
        return (x * 2 + z % 2) * 16 + y * 4 + z // 2 * 2 + core

    found = []
    for x in range(SIDE):
        for y in range(SIDE):
            for z in range(SIDE):
                for core in range(2):
                    found.append((flat(*source_of(x, y, z, core)), flat(x, y, z, core)))
    return found


SAME_CORE = [list(range(core, 16, 2)) for core in range(2)]
FROM_CORE = pairs(lambda x, y, z, core: (x, y, z, 1 - core))
FROM_UP = pairs(lambda x, y, z, core: (x, y + 1, z, core))
FROM_DOWN = pairs(lambda x, y, z, core: (x, y - 1, z, core))
FROM_ACROSS = pairs(lambda x, y, z, core: (x, y, 3 - z, core))


def take(values, found):
    return lax.ppermute(values, AXES, found)


def pack_kernel(place_ref, q_ref, k_ref, v_ref, mine_ref, other_ref):
    width = q_ref.shape[1]
    head_dim = width // HEADS

    def columns(core):
        cols = [slice(head * head_dim, (head + 1) * head_dim) for head in range(core, HEADS, 2)]
        return jnp.concatenate([ref[:, col] for ref in (q_ref, v_ref, k_ref) for col in cols], axis=1)

    first, second = columns(0), columns(1)
    core = jnp.full(first.shape, place_ref[3], jnp.int32) == 0
    mine_ref[...] = jnp.where(core, first.astype(F32), second.astype(F32)).astype(BF16)
    other_ref[...] = jnp.where(core, second.astype(F32), first.astype(F32)).astype(BF16)


def pack(place, q, k, v):
    depth, width = q.shape
    part = (depth, width // 2 * 3)
    return pl.pallas_call(
        pack_kernel,
        grid=(1,),
        out_shape=(jax.ShapeDtypeStruct(part, BF16),) * 2,
        in_specs=[SMEM] + [whole(q.shape)] * 3,
        out_specs=(whole(part),) * 2,
        compiler_params=params(),
        cost_estimate=cost(0, 2**21),
        name="pack",
    )(place, q, k, v)


def copies_kernel(in_ref, out_ref):
    out_ref[...] = jnp.broadcast_to(in_ref[...][None], out_ref.shape)


def copies_of(values, copies):
    out = (copies,) + values.shape
    return pl.pallas_call(
        copies_kernel,
        grid=(1,),
        out_shape=jax.ShapeDtypeStruct(out, BF16),
        in_specs=[whole(values.shape)],
        out_specs=whole(out),
        compiler_params=params(),
        cost_estimate=cost(0, 2**22),
        name="copies",
    )(values)


def norm_kernel(x_ref, gain_ref, segs_ref, out_ref, mean_ref):
    count, width = x_ref.shape
    segs = segs_ref[...]
    marks = (segs == lax.broadcasted_iota(jnp.int32, (128, count), 0) % IMG_DEV).astype(F32)
    out_ref[:, width:] = marks.T.astype(BF16)

    def one(i, _):
        rows = pl.ds(pl.multiple_of(i * 128, 128), 128)
        xf = x_ref[rows, :].astype(F32)
        centre = xf - jnp.mean(xf, axis=1, keepdims=True)
        spread = jnp.mean(centre * centre, axis=1, keepdims=True)
        out_ref[rows, :width] = (centre * lax.rsqrt(spread + 1e-06) * gain_ref[...]).astype(BF16)
        return 0

    lax.fori_loop(0, count // 128, one, 0)
    member = marks[:IMG_DEV]
    total = jnp.sum(member, axis=1, keepdims=True)
    mean_ref[...] = jnp.dot(member.astype(BF16), x_ref[...], preferred_element_type=F32) / total


def norm(x, gain, segs):
    count, width = x.shape
    return pl.pallas_call(
        norm_kernel,
        grid=(1,),
        out_shape=(
            jax.ShapeDtypeStruct((count, width + 128), BF16),
            jax.ShapeDtypeStruct((IMG_DEV, width), F32),
        ),
        in_specs=[whole(x.shape), whole((1, width)), whole(segs.shape)],
        out_specs=(whole((count, width + 128)), whole((IMG_DEV, width))),
        compiler_params=params(),
        cost_estimate=cost(0, 2**24),
        name="norm",
    )(x, gain.reshape(1, width), segs)


def split(values):
    high = values.astype(BF16)
    return jnp.concatenate([high, (values - high.astype(F32)).astype(BF16)], axis=0)


def join(values):
    half = values.shape[0] // 2
    return values[:half] + values[half:]


def attend_kernel(place_ref, window_ref, segs_ref, normed_hbm, *refs):
    shards, (context_ref, normed_ref, weight_s, qvk_s, sems) = refs[:-5], refs[-5:]
    count = normed_ref.shape[0]
    width = weight_s.shape[0]
    half = width // 2
    head_dim = width // HEADS
    shift = half // 128 * 128

    chunk = count // PROJECT_CHUNKS

    copies = []
    for at, shard in enumerate(shards):
        whole = min(at, 7)
        row = place_ref[4 + whole]
        if at >= 7:
            row = row + (at - 7) * shard.shape[0]
        rows = pl.ds(pl.multiple_of(row, 16), shard.shape[0])
        copies.append(pltpu.make_async_copy(shard, weight_s.at[rows, :], sems.at[at]))
    for copy in copies:
        copy.start()

    def normed_copy(i):
        rows = pl.ds(pl.multiple_of(i * chunk, chunk), chunk)
        return pltpu.make_async_copy(normed_hbm.at[rows, :], normed_ref.at[rows, :], sems.at[len(shards) + i])

    for i in range(PROJECT_CHUNKS):
        normed_copy(i).start()
    for copy in copies:
        copy.wait()

    lanes = lax.broadcasted_iota(jnp.int32, (1, 3 * half), 1)
    scale = jnp.where(lanes < half, math.log2(math.e) / math.sqrt(head_dim), 1.0).astype(F32)

    def project(i, _):
        normed_copy(i).wait()
        rows = pl.ds(pl.multiple_of(i * chunk, chunk), chunk)
        out = jnp.dot(normed_ref[rows, :width], weight_s[...], preferred_element_type=F32)
        qvk_s[rows, : 3 * half] = (out * scale).astype(BF16)
        return 0

    lax.fori_loop(0, PROJECT_CHUNKS, project, 0)
    lane = lax.broadcasted_iota(jnp.int32, (1, 256), 1)

    def span(low):
        base = low // 128 * 128
        wide = 128 if low + head_dim <= base + 128 else 256
        mine = (lane[:, :wide] >= low - base) & (lane[:, :wide] < low - base + head_dim)
        return base, wide, mine

    def block(at, blocks, first):
        qr = pl.ds(pl.multiple_of(at * QUERY_ROWS, QUERY_ROWS), QUERY_ROWS)
        kr = pl.ds(pl.multiple_of(first * KEY_ROWS, KEY_ROWS), blocks * KEY_ROWS)
        query_mark = normed_ref[qr, width:]
        query_mark = jnp.concatenate([query_mark, query_mark], axis=1)
        key_mark = ((normed_ref[kr, width:].astype(F32) - 1.0) * -MASKED).astype(BF16)
        key_mark = jnp.concatenate([key_mark, key_mark], axis=1)
        for head in range(HEADS // 2):
            base, wide, mine = span(head * head_dim)
            queries = jnp.where(mine, qvk_s[qr, base : base + wide], query_mark[:, :wide])
            base += 2 * half
            keys = jnp.where(mine, qvk_s[kr, base : base + wide], key_mark[:, :wide])
            low = half + head * head_dim
            base, wide, mine = span(low)
            values = jnp.where(mine, qvk_s[kr, base : base + wide], jnp.ones((), BF16))
            scores = lax.dot_general(queries, keys, (((1,), (1,)), ((), ())), preferred_element_type=F32)
            top = jnp.max(scores, axis=1, keepdims=True)
            probs = jnp.exp2(scores - top).astype(BF16)
            out = jnp.dot(probs, values, preferred_element_type=F32)
            spare = 0 if low > base else wide - 1
            out = (out * (1.0 / out[:, spare : spare + 1])).astype(BF16)
            cols = slice(base - shift, base - shift + wide)
            old = jnp.zeros((), BF16) if head == 0 else context_ref[qr, cols]
            context_ref[qr, cols] = jnp.where(mine, out, old)

    def one_block(at, _):
        first = window_ref[0, at]
        blocks = window_ref[1, at]
        for size in (3, 4, 5, 6):

            @pl.when((blocks == size) if size > 3 else (blocks <= 3))
            def _():
                block(at, size, jnp.minimum(first, count // KEY_ROWS - size))

        return 0

    lax.fori_loop(0, count // QUERY_ROWS, one_block, 0)
    member = (segs_ref[...] == lax.broadcasted_iota(jnp.int32, (IMG_DEV, count), 0)).astype(F32)
    total = jnp.sum(member, axis=1, keepdims=True)
    sums = jnp.dot(member.astype(BF16), context_ref[:count, :], preferred_element_type=F32)
    context_ref[count:, :] = split(sums / total)


def key_windows(segs):
    blocks = segs.reshape(-1, QUERY_ROWS)
    start = jnp.sum((segs < blocks[:, :1]).astype(jnp.int32), axis=1)
    end = jnp.sum((segs <= blocks[:, -1:]).astype(jnp.int32), axis=1)
    first = start // KEY_ROWS
    return jnp.stack([first, (end + KEY_ROWS - 1) // KEY_ROWS - first])


def attend(place, window, segs, normed, shards):
    count = normed.shape[0]
    width = normed.shape[1] - 128
    columns = width // 2 * 3
    across = width // 2 + 64
    return pl.pallas_call(
        attend_kernel,
        grid=(1,),
        out_shape=jax.ShapeDtypeStruct((count + 2 * IMG_DEV, across), BF16),
        in_specs=[SMEM] * 2 + [whole(segs.shape)] + [ANY] * (len(shards) + 1),
        out_specs=whole((count + 2 * IMG_DEV, across)),
        scratch_shapes=[
            pltpu.VMEM(normed.shape, BF16),
            pltpu.VMEM((width, columns), BF16),
            pltpu.VMEM((count, columns + 64), BF16),
            pltpu.SemaphoreType.DMA((len(shards) + PROJECT_CHUNKS,)),
        ],
        compiler_params=params(),
        cost_estimate=cost(10**10, 2**24),
        name="attend",
    )(place, window, segs, normed, *shards)


def pool_kernel(rows_mean_ref, own_ref, other_ref, own_weight_ref, other_weight_ref, unit_ref, out_ref):
    pooled = rows_mean_ref[...]
    for context_ref, weight_ref in ((own_ref, own_weight_ref), (other_ref, other_weight_ref)):
        pooled += join(jnp.dot(context_ref[:, 64:], weight_ref[...], preferred_element_type=F32))
    unit = pooled * lax.rsqrt(jnp.sum(pooled * pooled, axis=1, keepdims=True) + 1e-06)
    unit_ref[...] = unit
    out_ref[...] = jnp.broadcast_to(unit.astype(BF16)[None], out_ref.shape)


def pool(rows_mean, own, other, own_weight, other_weight, copies):
    images, width = rows_mean.shape
    last = own.shape[0] // (2 * images) - 1
    tail = pl.BlockSpec((2 * images, own.shape[1]), lambda i: (last, 0))
    weight = whole(own_weight.shape)
    return pl.pallas_call(
        pool_kernel,
        grid=(1,),
        out_shape=(jax.ShapeDtypeStruct((images, width), F32), jax.ShapeDtypeStruct((copies, images, width), BF16)),
        in_specs=[whole((images, width)), tail, tail, weight, weight],
        out_specs=(whole((images, width)), whole((copies, images, width))),
        compiler_params=params(),
        cost_estimate=cost(2**25, 2**22),
        name="pool",
    )(rows_mean, own, other, own_weight, other_weight)


def encode_kernel(x_ref, own_ref, other_ref, own_weight_ref, other_weight_ref, out_ref, weight_s):
    depth = own_ref.shape[1]

    @pl.when(pl.program_id(0) == 0)
    def _():
        for at, weight_ref in enumerate((own_weight_ref, other_weight_ref)):
            weight_s[at * depth : at * depth + 64, :] = jnp.zeros((64, weight_s.shape[1]), BF16)
            weight_s[at * depth + 64 : (at + 1) * depth, :] = weight_ref[...]

    context = jnp.concatenate([own_ref[...], other_ref[...]], axis=1)
    attended = jnp.dot(context, weight_s[...], preferred_element_type=F32)
    out_ref[...] = (x_ref[...].astype(F32) + attended).astype(BF16)


def encode(x, own, other, own_weight, other_weight):
    count, width = x.shape
    rows = 512
    block = pl.BlockSpec((rows, width), lambda i: (i, 0))
    half = pl.BlockSpec((rows, own.shape[1]), lambda i: (i, 0))
    weight = whole(own_weight.shape)
    return pl.pallas_call(
        encode_kernel,
        grid=(count // rows,),
        out_shape=jax.ShapeDtypeStruct((count, width), BF16),
        in_specs=[block, half, half, weight, weight],
        out_specs=block,
        scratch_shapes=[pltpu.VMEM((2 * own.shape[1], width), BF16)],
        compiler_params=params(),
        cost_estimate=cost(3 * 10**9, 2**24),
        name="encode",
    )(x, own, other, own_weight, other_weight)


def inverse_norm(values):
    return lax.rsqrt(jnp.sum(values * values, axis=1, keepdims=True) + 1e-06)


def sigmoid_coeffs(logits, diagonal):
    sign = jnp.where(diagonal, 1.0, -1.0).astype(F32)
    return -10.0 * sign * jax.nn.sigmoid(-sign * logits)


def text_kernel(place_ref, units_ref, mine_ref, theirs_ref, out_ref):
    units = units_ref[...]
    images, width = units.shape
    owners = mine_ref.shape[0]
    texts = owners * IMG_DEV
    row, core = place_ref[1], place_ref[3]
    for text_ref, at in ((mine_ref, core), (theirs_ref, 1 - core)):
        text = text_ref[:, row].astype(F32).reshape(texts, width)
        scale = inverse_norm(text)
        dots = lax.dot_general(text.astype(BF16), units, (((1,), (1,)), ((), ())), preferred_element_type=F32)
        image = lax.broadcasted_iota(jnp.int32, (texts, images), 1) - row * IMG_DEV
        index = lax.broadcasted_iota(jnp.int32, (texts, images), 0)
        index = index // IMG_DEV * 2 * IMG_DEV + index % IMG_DEV + (at - place_ref[2]) * IMG_DEV
        diagonal = (image == index) & (image >= 0) & (image < IMG_DEV)
        coeffs = sigmoid_coeffs(10.0 * dots * scale - 3.0, diagonal)
        term = join(jnp.dot(split(coeffs), units, preferred_element_type=F32))
        out_ref[:, at] = term.reshape(owners, IMG_DEV, width).astype(BF16)


def text_terms(place, units, mine, theirs):
    images, width = units.shape
    out = (mine.shape[0], 2, IMG_DEV, width)
    return pl.pallas_call(
        text_kernel,
        grid=(1,),
        out_shape=jax.ShapeDtypeStruct(out, BF16),
        in_specs=[SMEM, whole((images, width)), whole(mine.shape), whole(mine.shape)],
        out_specs=whole(out),
        compiler_params=params(40),
        cost_estimate=cost(2**26, 2**21),
        name="text_terms",
    )(place, units, mine, theirs)


def image_kernel(place_ref, unit_ref, mine_ref, theirs_ref, out_ref):
    unit = unit_ref[...]
    images, width = unit.shape
    grad = jnp.zeros(unit.shape, F32)
    for text_ref, low in ((mine_ref, place_ref[0]), (theirs_ref, -1)):
        text = text_ref[...]
        texts = text.shape[0]
        scale = inverse_norm(text.astype(F32))
        dots = lax.dot_general(text, split(unit), (((1,), (1,)), ((), ())), preferred_element_type=F32)
        dots = dots[:, :images] + dots[:, images:]
        image = lax.broadcasted_iota(jnp.int32, (texts, images), 1) + low * images
        diagonal = image == lax.broadcasted_iota(jnp.int32, (texts, images), 0)
        coeffs = sigmoid_coeffs(10.0 * dots * scale - 3.0, diagonal) * scale
        grad += join(jnp.dot(split(coeffs.T), text, preferred_element_type=F32))
    out_ref[...] = grad


def image_gradient(place, unit, mine, theirs):
    return pl.pallas_call(
        image_kernel,
        grid=(1,),
        out_shape=jax.ShapeDtypeStruct(unit.shape, F32),
        in_specs=[SMEM, whole(unit.shape), whole(mine.shape), whole(mine.shape)],
        out_specs=whole(unit.shape),
        compiler_params=params(),
        cost_estimate=cost(2**28, 2**22),
        name="image_gradient",
    )(place, unit, mine, theirs)


def gather_weights(own, first, second):
    up, down, across, beside = lax.optimization_barrier(
        (take(own, FROM_UP), take(own, FROM_DOWN), take(own, FROM_ACROSS), first())
    )
    far, across_up, across_down, beside = lax.optimization_barrier(
        (take(up, FROM_UP), take(up, FROM_ACROSS), take(across, FROM_DOWN), second(beside))
    )
    third = own.shape[0] // 3
    last = [
        take(far[:third], FROM_ACROSS),
        take(across_up[third : 2 * third], FROM_UP),
        take(across_down[2 * third :], FROM_DOWN),
    ]
    return [own, up, down, far, across, across_up, across_down] + last, beside


def body(
    patch_rows,
    segment_ids,
    norm_gain,
    query_weight,
    key_weight,
    value_weight,
    out_weight,
    text_embeds,
):
    count, width = patch_rows.shape
    n_row = lax.axis_size("row")
    n_col = lax.axis_size("col")
    row_at = lax.axis_index("row")
    col_at = lax.axis_index("col")
    core = col_at % 2
    y_at = col_at // 4
    z_hi = col_at // 2 % 2
    depth = query_weight.shape[0] * 2
    steps = [(0, 0), (1, 0), (-1, 0), (2, 0), (0, 1), (1, 1), (-1, 1), (2, 1)]
    firsts = [((y_at + dy) % SIDE * 2 + (z_hi + dz) % 2) * depth for dy, dz in steps]
    place = jnp.stack([col_at // 2 * n_row + row_at, row_at, col_at, core] + firsts).astype(jnp.int32)
    texts = text_embeds.shape[0]

    owners = n_col // 2
    mine, other = pack(place, query_weight, key_weight, value_weight)
    theirs = take(other, FROM_CORE)
    other_segs = take(segment_ids, FROM_CORE)
    own = jnp.where(core == 0, jnp.concatenate([mine, theirs]), jnp.concatenate([theirs, mine]))
    own, rows, other_segs, out_rows, own_text = lax.optimization_barrier(
        (own, patch_rows, other_segs, out_weight, text_embeds)
    )

    def first():
        column_text = lax.all_to_all(copies_of(own_text, n_row), "row", 0, 0)
        return norm(rows, norm_gain, segment_ids), column_text

    def second(beside):
        (normed, rows_mean), column_text = beside
        text_copies = copies_of(column_text.reshape(n_row * texts, width), owners)
        window = key_windows(segment_ids)
        return normed, take(normed, FROM_CORE), rows_mean, text_copies, copies_of(out_rows, owners), window

    shards, beside = gather_weights(own, first, second)
    normed, other_normed, rows_mean, text_copies, out_copies, window = beside
    own_out = lax.all_to_all(out_copies, "col", 0, 0, axis_index_groups=SAME_CORE)
    for_other = attend(place, key_windows(other_segs), other_segs, other_normed, shards)
    for_other, own_out = lax.optimization_barrier((for_other, own_out))
    context_other = take(for_other, FROM_CORE)
    own_out = own_out.reshape(width // 2, width)
    other_out = take(own_out, FROM_CORE)
    own_text = lax.all_to_all(text_copies, "col", 0, 0, axis_index_groups=SAME_CORE)
    own_text = own_text.reshape(owners, n_row, texts, width)
    context_own = attend(place, window, segment_ids, normed, shards)
    unit, units = pool(rows_mean, context_own, context_other, own_out, other_out, n_row)
    units, own_text = lax.optimization_barrier((units, own_text))
    other_text = take(own_text, FROM_CORE)
    units = lax.all_to_all(units, "row", 0, 0)
    encoded = encode(patch_rows, context_own, context_other, own_out, other_out)
    units, encoded = lax.optimization_barrier((units, encoded))
    terms = text_terms(place, units.reshape(n_row * IMG_DEV, width), own_text, other_text)
    terms, unit = lax.optimization_barrier((terms, unit))
    terms = lax.all_to_all(terms.reshape(n_col, texts, width), "col", 0, 0)
    every = owners * n_row * texts
    image_grad = image_gradient(place, unit, own_text.reshape(every, width), other_text.reshape(every, width))
    return (encoded, image_grad, jnp.sum(terms.astype(F32), axis=0))


def solution(mesh):
    return jax.shard_map(
        body,
        mesh=mesh,
        in_specs=(
            P(("row", "col"), None),
            P(("row", "col"), None),
            P(),
            P("col", None),
            P("col", None),
            P("col", None),
            P("col", None),
            P(("row", "col"), None),
        ),
        out_specs=(P(("row", "col"), None), P(("row", "col"), None), P(("row", "col"), None)),
        check_vma=False,
    )
```
